128 devices in a mesh: grp: 32 (over y, x, core), blk: 4 (over z).
Axes of the slice: x: 4, y: 4, z: 4, core: 2. Of those that a mesh axis runs over, the one named last changes fastest.
Arguments:
- embeddings: bfloat16 [131072, 1024], P(('grp', 'blk')), may hold values from -6 to 6
- doc_group: int32 [131072, 1], P(('grp', 'blk')), may hold values from 0 to 31; in each aligned block of 1024 rows (0 to 1023, 1024 to 2047, ...) at most 48 rows name the same one
- doc_cluster: int32 [131072], P(('grp', 'blk')), may hold values from 0 to 1
Outputs:
- max_sim: float32 [131072], P(('grp', 'blk'))
The draws below stay inside these ranges and needn't reach their ends.
Inputs may be any that keep to these rules, and one draw needn't show every extreme that they name: `doc_group`: in each aligned block of 1024 rows (the rows of one device) no subgroup is named by more than 48 rows, a bound that some block reaches.
All inputs are finite; a program needn't handle non-finite values.
Results may differ from the reference program's by a relative error of at most 0.0013.
Values may be sent and summed in bfloat16 or wider, within the bound.
A program may use at most 64 MiB of HBM per device.

```python
import math
import jax
import jax.numpy as jnp
import numpy as np
from jax import lax

D = 1024
ROWS = 1024
CL_GRP = 2
CAP = 48
TOKENS = 131072
N_GRP = 32


def place_ends(array, rng, smallest, largest):
    extent = array.shape
    place = [jax.random.randint(jax.random.fold_in(rng, axis), (), 0, extent[axis]) for axis in range(len(extent))]
    array = array.at[tuple(place)].set(smallest)
    longest = extent.index(max(extent))
    place[longest] = (place[longest] + 1) % extent[longest]
    return array.at[tuple(place)].set(largest)


def block_levels(rng, extent, cuts, smallest, top_value):
    factor_of, own = 1.0, jax.random.fold_in(rng, 6)
    for dim, parts in cuts:
        heights = jnp.exp(jax.random.uniform(jax.random.fold_in(own, dim), (parts,), jnp.float32, smallest / len(cuts), top_value / len(cuts)))
        factor_of = factor_of * jnp.repeat(heights, extent[dim] // parts).reshape([-1 if axis == dim else 1 for axis in range(len(extent))])
    return factor_of


def rank_table(count, lean):
    portions = [(1 << 20) // math.isqrt(standing ** lean) + 1 for standing in range(1, count + 1)]
    spread = 1 + sum(portions) // (1 << 30)
    return np.cumsum(np.array([max(1, weight // spread) for weight in portions]))


def skewed_ids(rng, shape, count, slope):
    table = rank_table(count, slope)
    lot = jax.random.randint(jax.random.fold_in(rng, 1), shape, 0, int(table[count - 1]))
    rank = jnp.searchsorted(jnp.asarray(table, jnp.int32), lot, side="right")
    return jax.random.permutation(jax.random.fold_in(rng, 2), count)[rank].astype(jnp.int32)


def assign_block(rng, own, number, rows, count, top, limit, skew):
    sequence = jax.random.permutation(rng, count)
    heavy_load, common = load_shares(count, rows * top, limit, skew, True), load_shares(count, rows * top, limit, skew, False)
    places = jnp.arange(count)

    def named(lengths, rotation):
        used = int((lengths > 0).sum())
        fixed = max(1, used // 4)
        moved = fixed + (places - fixed + rotation * (used - fixed)) % max(1, count - fixed)
        return jnp.zeros((count,), jnp.int32).at[sequence[jnp.where(places < fixed, places, moved)]].set(jnp.asarray(lengths, jnp.int32))

    lengths = jnp.where(number % 4 == 0, named(heavy_load, number // 4), named(common, number - number // 4 - 1))
    mixed = jax.random.permutation(jax.random.fold_in(own, 3), count)
    donor, taker = mixed[0:count // 2 * 2:2], mixed[1:count // 2 * 2:2]
    room = jnp.minimum(lengths[donor] - 1, limit - lengths[taker]) // 2
    room = jnp.where((donor == sequence[0]) | (taker == sequence[0]) | (lengths[taker] == 0), 0, jnp.maximum(room, 0))
    moved = jax.random.randint(jax.random.fold_in(own, 4), (count // 2,), 0, 1 << 20) % (room + 1)
    lengths = lengths.at[donor].add(-moved).at[taker].add(moved)
    items = jnp.searchsorted(jnp.cumsum(lengths), jnp.arange(rows * top), side="right").astype(jnp.int32)
    grid = items.reshape(top, rows).T
    grid = grid[jax.random.permutation(jax.random.fold_in(own, 1), rows)]
    rotation = jax.random.randint(jax.random.fold_in(own, 2), (rows, 1), 0, top)
    return jnp.take_along_axis(grid, (jnp.arange(top)[None, :] + rotation) % top, axis=1)


def load_shares(amount, total, limit, skew, full):
    loads = [(1 << 20) // math.isqrt(standing ** skew) + 1 for standing in range(1, amount + 1)]
    largest = limit if full else min(limit, max(-(-total // amount), total * loads[0] // sum(loads)))
    least = 1 if total - largest >= amount - 1 else 0
    given, surplus = [largest] + [least] * (amount - 1), total - largest - least * (amount - 1)
    while surplus > 0:
        free = [i for i in range(1, amount) if given[i] < largest] or [i for i in range(1, amount) if given[i] < limit]
        pool, budget = sum([loads[i] for i in free]), surplus
        for i in free:
            extra = min(limit - given[i], max(1, budget * loads[i] // pool), surplus)
            given[i] = given[i] + extra
            surplus = surplus - extra
    return np.array(given)


def scatter_about(rng, dims, deviation, limit, cuts=(), kind=jnp.bfloat16):
    array = jax.random.normal(rng, dims, jnp.float32) * deviation
    if len(cuts) > 0:
        array = block_levels(rng, dims, cuts, -0.22, 0.18) * array
    return jnp.clip(array, min=-limit, max=limit).astype(kind)


def setup_inputs(seed: int = 0) -> dict:
    streams_of = jax.random.split(jax.random.key(seed), 4)
    embeddings = scatter_about(streams_of[0], (TOKENS, D), 1.0, 6.0, ((0, 128),))
    doc_group_keys = jax.random.split(jax.random.fold_in(streams_of[1], 1), TOKENS // ROWS)
    doc_group_turns = jax.random.permutation(jax.random.fold_in(streams_of[1], 3), TOKENS // ROWS)
    doc_group = jax.vmap(lambda own, number: assign_block(jax.random.fold_in(streams_of[1], 2), own, number, ROWS, N_GRP, 1, CAP, 2))(doc_group_keys, doc_group_turns).reshape((TOKENS, 1))
    doc_cluster = place_ends(skewed_ids(streams_of[2], (TOKENS,), CL_GRP, 1), jax.random.fold_in(streams_of[2], 3), 0, CL_GRP - 1).astype(jnp.int32)
    return dict(embeddings=embeddings, doc_group=doc_group, doc_cluster=doc_cluster)


def reference(embeddings, doc_group, doc_cluster):
    values = embeddings.astype(jnp.float32)
    unit = (values / jnp.sqrt(lax.optimization_barrier(jnp.sum(values * values, axis=1, keepdims=True)) + 1e-06)).astype(jnp.bfloat16)
    labels = (doc_group[:, 0] * CL_GRP + doc_cluster).astype(jnp.int32)
    order = jnp.argsort(labels, stable=True).astype(jnp.int32)
    sorted_keys = labels[order]
    sorted_unit = unit[order]
    total = sorted_keys.shape[0]
    width_blk = 256
    count_blk = total // width_blk
    first = jnp.searchsorted(sorted_keys, sorted_keys, side='left').astype(jnp.int32)
    last = jnp.searchsorted(sorted_keys, sorted_keys, side='right').astype(jnp.int32)

    def one_block(index):
        start = (index * width_blk).astype(jnp.int32)
        rows = lax.dynamic_slice_in_dim(sorted_unit, start, width_blk, 0)
        row_keys = lax.dynamic_slice_in_dim(sorted_keys, start, width_blk, 0)
        row_pos = start + jnp.arange(width_blk, dtype=jnp.int32)
        lower = first[start] // width_blk
        upper = (last[start + width_blk - 1] - 1) // width_blk + 1

        def step(col, best):
            col_start = (col * width_blk).astype(jnp.int32)
            cols = lax.dynamic_slice_in_dim(sorted_unit, col_start, width_blk, 0)
            col_keys = lax.dynamic_slice_in_dim(sorted_keys, col_start, width_blk, 0)
            col_pos = col_start + jnp.arange(width_blk, dtype=jnp.int32)
            sims = lax.dot_general(rows, cols, (((1,), (1,)), ((), ())), preferred_element_type=jnp.float32)
            mask = (row_keys[:, None] == col_keys[None, :]) & (row_pos[:, None] != col_pos[None, :])
            return jnp.maximum(best, lax.optimization_barrier(jnp.max(jnp.where(mask, sims, jnp.float32(-1.0)), axis=1)))
        return lax.fori_loop(lower, upper, step, jnp.full((width_blk,), -1.0, jnp.float32))
    result = lax.map(one_block, jnp.arange(count_blk, dtype=jnp.int32)).reshape(total)
    return jnp.zeros((total,), jnp.float32).at[order].set(result)
```

```python
import functools

import jax
import jax.numpy as jnp
from jax import lax
from jax.experimental import pallas as pl
from jax.experimental.pallas import tpu as pltpu
from jax.sharding import PartitionSpec as P

MESH = pl.DeviceIdType.MESH
F32, BF16, I32 = jnp.float32, jnp.bfloat16, jnp.int32
GROUPS, CAP = 32, 48
HALF = 16 * CAP
LAG = 5
TASKS = 11


def dot_nt(a, b):
    return lax.dot_general(a, b, (((1,), (1,)), ((), ())), preferred_element_type=F32)


def dot_nn(a, b):
    return lax.dot_general(a, b, (((1,), (0,)), ((), ())), preferred_element_type=F32)


def dot_tn(a, b):
    return lax.dot_general(a, b, (((0,), (0,)), ((), ())), preferred_element_type=F32)


def pick(index, values):
    out = values[-1]
    for i in range(len(values) - 2, -1, -1):
        out = jnp.where(index == i, values[i], out)
    return out


def kernel(
    emb_ref, grp_ref, clu_ref, out_ref,
    unit, send, csend, docs, cnts, lab_c, lab_r, sims, row_best, col_best,
    zsend_a, zsend_f, zsend_b, zrecv_a, zrecv_f, zrecv_b, res, ret,
    ss, sr, cs, cr, fs, fr, gs, gr, hs, hr, zs, zr, rs, rr,
):
    g = lax.axis_index("grp")
    z = lax.axis_index("blk")
    y, x, c = g // 8, lax.rem(g // 2, 4), lax.rem(g, 2)
    m = jnp.where(c == 0, z, lax.rem(4 - z, 4))

    def along_z(d):
        return (g, lax.rem(z + jnp.where(c == 0, d, 4 - d), 4))

    def at_offset(k, sign):
        off = lax.rem(7 * k, 32)
        dy, dx, dc = off // 8, lax.rem(off // 2, 4), lax.rem(off, 2)
        ty, tx = lax.rem(y + 4 + sign * dy, 4), lax.rem(x + 4 + sign * dx, 4)
        return ((ty * 4 + tx) * 2 + lax.rem(c + dc, 2), z)

    def remote(src, dst, s_sem, r_sem, target):
        return pltpu.make_async_remote_copy(
            src_ref=src, dst_ref=dst, send_sem=s_sem, recv_sem=r_sem,
            device_id=target, device_id_type=MESH,
        )

    def first_hop(k):
        return remote(send.at[k], docs.at[k], ss.at[k], sr.at[k], at_offset(k, 1))

    def first_counts(k):
        return remote(csend.at[k], cnts.at[k], cs.at[k], cr.at[k], at_offset(k, 1))

    def adjacent(k):
        return remote(docs.at[k], docs.at[32 + k], fs.at[k], fr.at[k], along_z(1))

    def further(k):
        return remote(docs.at[32 + k], docs.at[64 + k], gs.at[k], gr.at[k], along_z(1))

    def back(k):
        return remote(docs.at[k], docs.at[64 + k], gs.at[k], gr.at[k], along_z(3))

    def adjacent_counts(h):
        return remote(
            cnts.at[pl.ds(16 * h, 16)], cnts.at[pl.ds(32 + 16 * h, 16)], hs.at[h], hr.at[h], along_z(1)
        )

    def further_counts():
        return remote(cnts.at[pl.ds(32, 16)], cnts.at[pl.ds(64, 16)], hs.at[2], hr.at[2], along_z(1))

    def back_counts():
        return remote(cnts.at[pl.ds(16, 16)], cnts.at[pl.ds(80, 16)], hs.at[3], hr.at[3], along_z(3))

    sends_further = (m == 1) | (m == 2)
    gets_further = m >= 2
    sends_back = m < 2
    gets_back = (m == 3) | (m == 0)

    zrecv_a[...] = jnp.full_like(zrecv_a, -1.0)
    zrecv_f[...] = jnp.full_like(zrecv_f, -1.0)
    zrecv_b[...] = jnp.full_like(zrecv_b, -1.0)

    barrier = pltpu.get_barrier_semaphore()

    def greet(k, carry):
        pl.semaphore_signal(barrier, 1, device_id=at_offset(k, -1), device_id_type=MESH)
        return carry

    lax.fori_loop(1, 32, greet, 0)
    for d in (1, 2, 3):
        pl.semaphore_signal(barrier, 1, device_id=along_z(d), device_id_type=MESH)

    for b in range(4):
        rows = emb_ref[256 * b : 256 * b + 256, :].astype(F32)
        norm = jnp.sqrt(jnp.sum(rows * rows, axis=1, keepdims=True) + 1e-06)
        unit[256 * b : 256 * b + 256, :] = (rows * (1.0 / norm)).astype(BF16)

    grp = grp_ref[...]
    gy, gx, gc = grp // 8, (grp // 2) & 3, grp & 1
    off = ((gy - y) & 3) * 8 + ((gx - x) & 3) * 2 + ((gc - c) & 1)
    place = (off * 23) & 31
    clu = clu_ref[...]
    kind = place * 2 + clu
    mine = (lax.broadcasted_iota(I32, (64, 1024), 0) == kind).astype(F32)
    mine_b = mine.astype(BF16)
    before = (
        lax.broadcasted_iota(I32, (256, 256), 0) < lax.broadcasted_iota(I32, (256, 256), 1)
    ).astype(F32).astype(BF16)
    offset = jnp.zeros((64, 1), F32)
    ranks = []
    for b in range(4):
        part = mine[:, 256 * b : 256 * b + 256]
        within = dot_nn(mine_b[:, 256 * b : 256 * b + 256], before) + offset
        ranks.append(jnp.sum(part * within, axis=0, keepdims=True))
        offset = offset + jnp.sum(part, axis=1, keepdims=True)
    rank = jnp.concatenate(ranks, axis=1).astype(I32)
    rank = jnp.where(clu == 0, rank, CAP - 1 - rank)
    slot = place * CAP + rank

    same = (lax.broadcasted_iota(I32, (256, 1024), 0) // 4 == kind).astype(F32)
    total = jnp.sum(same, axis=1, keepdims=True)
    csend[...] = jnp.broadcast_to(total, (256, 128)).reshape(32, 8, 128)

    def start_first(k, carry):
        first_hop(k).start()
        first_counts(k).start()
        return carry

    for b in range(4):
        here = lax.broadcasted_iota(I32, (8 * CAP, 1024), 0) + 8 * CAP * b == slot
        picked = dot_nn(here.astype(F32).astype(BF16), unit[...]).astype(BF16)
        send[8 * b : 8 * b + 8] = picked.reshape(8, CAP, 1024)
        if b == 0:
            docs[0] = send[0]
            cnts[0] = csend[0]
            pl.semaphore_wait(barrier, 34)
        lax.fori_loop(max(1, 8 * b), 8 * b + 8, start_first, 0)

    row_best[...] = jnp.full_like(row_best, -1.0)
    col_best[...] = jnp.full_like(col_best, -1.0)

    def relay_further(k):
        adjacent(k).wait_recv()

        @pl.when(sends_further & (k < 16))
        def _():
            further(k).start()

    def relay(k, carry):
        @pl.when(k >= 1)
        def _():
            first_hop(k).wait_recv()
            first_counts(k).wait_recv()

        adjacent(k).start()

        @pl.when(sends_back & (k >= 16))
        def _():
            back(k).start()

        @pl.when(k >= LAG)
        def _():
            relay_further(k - LAG)

        return carry

    def late(k, carry):
        relay_further(k)
        return carry

    def wait_opposite(k, carry):
        further(k).wait_recv()
        return carry

    def prepare(h):
        lane_row = lax.broadcasted_iota(I32, (CAP, 128), 0).astype(F32)
        for k in range(16):
            n0 = cnts[16 * h + k, 0:1, :]
            n1 = cnts[16 * h + k, 4:5, :]
            lab = jnp.where(lane_row < n0, 0.0, jnp.where(lane_row >= CAP - n1, 1.0, -1.0))
            lab_c[HALF * h + CAP * k : HALF * h + CAP * k + CAP, :] = lab
        for b in range(6):
            at = HALF * h + 128 * b
            lab_r[:, at : at + 128] = lab_c[at : at + 128, :].T[0:8, :]

    def step(j, carry):
        lo = pick(j, [0, 16, 23, 28, 32])
        hi = pick(j, [16, 23, 28, 32, 32])
        lax.fori_loop(lo, hi, relay, 0)

        @pl.when(j == 0)
        def _():
            adjacent_counts(0).start()
            prepare(0)

        @pl.when(j == 1)
        def _():
            adjacent_counts(0).wait_recv()

            @pl.when(sends_further)
            def _():
                further_counts().start()

            prepare(2)

        @pl.when((j == 2) & gets_further)
        def _():
            lax.fori_loop(0, 16, wait_opposite, 0)
            further_counts().wait_recv()
            prepare(4)

        @pl.when(j == 3)
        def _():
            adjacent_counts(1).start()

            @pl.when(sends_back)
            def _():
                back_counts().start()

            prepare(1)

        @pl.when(j == 7)
        def _():
            lax.fori_loop(32 - LAG, 32, late, 0)
            adjacent_counts(1).wait_recv()
            prepare(3)

        @pl.when((j == 9) & gets_back)
        def _():
            lax.fori_loop(16, 32, wait_opposite, 0)
            back_counts().wait_recv()
            prepare(5)

        r = pick(j, [0, 0, 0, 0, 1, 1, 1, 0, 1, 2, 3])
        q = pick(j, [0, 2, 4, 1, 1, 2, 4, 3, 3, 5, 5])
        wanted = ((q != 4) | gets_further) & ((q != 5) | gets_back)

        @pl.when(wanted)
        def _():
            left = docs[pl.ds(16 * r, 16)].reshape(HALF, 1024)
            right = docs[pl.ds(16 * q, 16)].reshape(HALF, 1024)
            sims[...] = dot_nt(left, right)

            @pl.when(r == q)
            def _():
                eye = lax.broadcasted_iota(I32, (128, 128), 0) == lax.broadcasted_iota(I32, (128, 128), 1)
                for b in range(6):
                    at = slice(128 * b, 128 * b + 128)
                    sims[at, at] = jnp.where(eye, -1.0, sims[at, at])

            r0 = pl.multiple_of(r * HALF, HALF)
            q0 = pl.multiple_of(q * HALF, HALF)
            labels = lab_c[pl.ds(r0, HALF), :]
            best = row_best[pl.ds(r0, HALF), :]
            for b in range(6):
                tile = sims[:, 128 * b : 128 * b + 128]
                cols = pl.ds(pl.multiple_of(q0 + 128 * b, 128), 128)
                tile = jnp.where(labels == lab_r[0:1, cols], tile, -1.0)
                best = jnp.maximum(best, tile)
                top = jnp.max(tile.reshape(HALF // 8, 8, 128), axis=0)
                col_best[:, cols] = jnp.maximum(col_best[:, cols], top)
            row_best[pl.ds(r0, HALF), :] = best

        return carry

    lax.fori_loop(0, TASKS, step, 0)

    def cols_of(h):
        return jnp.max(col_best[:, HALF * h : HALF * h + HALF], axis=0, keepdims=True)

    def both_of(h):
        parts = []
        for b in range(6):
            at = HALF * h + 128 * b
            parts.append(jnp.max(row_best[at : at + 128, :].T, axis=0, keepdims=True))
        return jnp.maximum(jnp.concatenate(parts, axis=1), cols_of(h))

    to_left = remote(zsend_a, zrecv_a, zs.at[0], zr.at[0], along_z(3))
    to_far = remote(zsend_f, zrecv_f, zs.at[1], zr.at[1], along_z(2))
    to_right = remote(zsend_b, zrecv_b, zs.at[2], zr.at[2], along_z(1))
    zsend_a[:, 0:HALF] = both_of(2)
    zsend_a[:, HALF : 2 * HALF] = both_of(3)
    to_left.start()

    @pl.when(gets_further)
    def _():
        zsend_f[...] = cols_of(4)
        to_far.start()

    @pl.when(gets_back)
    def _():
        zsend_b[...] = cols_of(5)
        to_right.start()

    res[:, 2 * HALF :] = jnp.full((1, 128), -1.0, F32)
    res[:, 0:HALF] = both_of(0)
    res[:, HALF : 2 * HALF] = both_of(1)

    @pl.when(m < 2)
    def _():
        to_far.wait_recv()
        to_right.wait_recv()

    to_left.wait_recv()
    others = jnp.concatenate([zrecv_f[...], zrecv_b[...]], axis=1)
    others = jnp.maximum(others, zrecv_a[...])
    res[:, 0 : 2 * HALF] = jnp.maximum(res[:, 0 : 2 * HALF], others)

    def answer(k):
        at = pl.multiple_of(CAP * k // 128 * 128, 128)
        return remote(res.at[:, pl.ds(at, 256)], ret.at[k], rs.at[k], rr.at[k], at_offset(k, -1))

    def start_answer(k, carry):
        answer(k).start()
        return carry

    lax.fori_loop(1, 32, start_answer, 0)
    ret[0] = res[:, 0:256]

    def sent(k, carry):
        @pl.when(k >= 1)
        def _():
            first_hop(k).wait_send()
            first_counts(k).wait_send()

        adjacent(k).wait_send()

        @pl.when(sends_further & (k < 16))
        def _():
            further(k).wait_send()

        @pl.when(sends_back & (k >= 16))
        def _():
            back(k).wait_send()

        return carry

    lax.fori_loop(0, 32, sent, 0)
    adjacent_counts(0).wait_send()
    adjacent_counts(1).wait_send()
    to_left.wait_send()

    @pl.when(sends_further)
    def _():
        further_counts().wait_send()

    @pl.when(sends_back)
    def _():
        back_counts().wait_send()

    @pl.when(gets_further)
    def _():
        to_far.wait_send()

    @pl.when(gets_back)
    def _():
        to_right.wait_send()

    def answered(k, carry):
        answer(k).wait_recv()
        answer(k).wait_send()
        return carry

    lax.fori_loop(1, 32, answered, 0)
    table = jnp.concatenate([ret[k] for k in range(32)], axis=0)
    where = (lax.broadcasted_iota(I32, (32, 1024), 0) == place).astype(F32).astype(BF16)
    high = table.astype(BF16)
    rest = table - high.astype(F32)
    mid = rest.astype(BF16)
    low = (rest - mid.astype(F32)).astype(BF16)
    found = dot_tn(high, where) + dot_tn(mid, where) + dot_tn(low, where)
    lane = rank + ((place * CAP) & 127)
    hit = lax.broadcasted_iota(I32, (256, 1024), 0) == lane
    out_ref[...] = jnp.max(jnp.where(hit, found, -2.0), axis=0, keepdims=True)


def per_device(embeddings, doc_group, doc_cluster):
    vmem = pl.BlockSpec(memory_space=pltpu.VMEM)
    dma = pltpu.SemaphoreType.DMA
    out = pl.pallas_call(
        kernel,
        out_shape=jax.ShapeDtypeStruct((1, 1024), F32),
        in_specs=[vmem] * 3,
        out_specs=vmem,
        scratch_shapes=[
            pltpu.VMEM((1024, 1024), BF16),
            pltpu.VMEM((32, CAP, 1024), BF16),
            pltpu.VMEM((32, 8, 128), F32),
            pltpu.VMEM((96, CAP, 1024), BF16),
            pltpu.VMEM((96, 8, 128), F32),
            pltpu.VMEM((6 * HALF, 128), F32),
            pltpu.VMEM((8, 6 * HALF), F32),
            pltpu.VMEM((HALF, HALF), F32),
            pltpu.VMEM((4 * HALF, 128), F32),
            pltpu.VMEM((8, 6 * HALF), F32),
            pltpu.VMEM((1, 2 * HALF), F32),
            pltpu.VMEM((1, HALF), F32),
            pltpu.VMEM((1, HALF), F32),
            pltpu.VMEM((1, 2 * HALF), F32),
            pltpu.VMEM((1, HALF), F32),
            pltpu.VMEM((1, HALF), F32),
            pltpu.VMEM((1, 2 * HALF + 128), F32),
            pltpu.VMEM((32, 1, 256), F32),
            dma((32,)), dma((32,)), dma((32,)), dma((32,)),
            dma((32,)), dma((32,)), dma((32,)), dma((32,)),
            dma((4,)), dma((4,)), dma((3,)), dma((3,)), dma((32,)), dma((32,)),
        ],
        compiler_params=pltpu.CompilerParams(
            collective_id=0, has_side_effects=True, vmem_limit_bytes=56 << 20
        ),
        cost_estimate=pl.CostEstimate(flops=24_000_000_000, bytes_accessed=2_200_000, transcendentals=0),
    )(embeddings, doc_group.reshape(1, -1), doc_cluster.reshape(1, -1))
    return out.reshape(-1)


def solution(mesh):
    in_specs = (P(("grp", "blk"), None), P(("grp", "blk"), None), P(("grp", "blk")))
    out_specs = P(("grp", "blk"))
    return jax.shard_map(
        per_device, mesh=mesh, in_specs=in_specs, out_specs=out_specs, check_vma=False
    )
```

```python
import functools

import jax
import jax.numpy as jnp
from jax import lax
from jax.experimental import pallas as pl
from jax.experimental.pallas import tpu as pltpu
from jax.sharding import PartitionSpec as P

MESH = pl.DeviceIdType.MESH
F32, BF16, I32 = jnp.float32, jnp.bfloat16, jnp.int32
GROUPS, CAP = 32, 48
HALF = 16 * CAP
LAG = 5
QUARTER = 8 * CAP
TASKS = 22
UNTIL = [16, 17, 19, 21, 24, 25, 28, 30, 32]


def dot_nt(a, b):
    return lax.dot_general(a, b, (((1,), (1,)), ((), ())), preferred_element_type=F32)


def dot_nn(a, b):
    return lax.dot_general(a, b, (((1,), (0,)), ((), ())), preferred_element_type=F32)


def dot_tn(a, b):
    return lax.dot_general(a, b, (((0,), (0,)), ((), ())), preferred_element_type=F32)


def pick(index, values):
    out = values[-1]
    for i in range(len(values) - 2, -1, -1):
        out = jnp.where(index == i, values[i], out)
    return out


def kernel(
    emb_ref, grp_ref, clu_ref, out_ref,
    emb, unit, send, csend, docs, cnts, lab_c, lab_r, sims, row_best, col_best,
    rows_r, zsend_a, zsend_f, zsend_b, zrecv_a, zrecv_f, zrecv_b, res, ret,
    ls, ss, sr, cs, cr, fs, fr, gs, gr, hs, hr, zs, zr, rs, rr,
):
    g = lax.axis_index("grp")
    z = lax.axis_index("blk")
    y, x, c = g // 8, lax.rem(g // 2, 4), lax.rem(g, 2)
    m = jnp.where(c == 0, z, lax.rem(4 - z, 4))

    def along_z(d):
        return (g, lax.rem(z + jnp.where(c == 0, d, 4 - d), 4))

    def at_offset(k, sign):
        off = lax.rem(11 * k, 32)
        dy, dx, dc = off // 8, lax.rem(off // 2, 4), lax.rem(off, 2)
        ty, tx = lax.rem(y + 4 + sign * dy, 4), lax.rem(x + 4 + sign * dx, 4)
        return ((ty * 4 + tx) * 2 + lax.rem(c + dc, 2), z)

    def remote(src, dst, s_sem, r_sem, target):
        return pltpu.make_async_remote_copy(
            src_ref=src, dst_ref=dst, send_sem=s_sem, recv_sem=r_sem,
            device_id=target, device_id_type=MESH,
        )

    def first_hop(k):
        return remote(send.at[k], docs.at[k], ss.at[k], sr.at[k], at_offset(k, 1))

    def first_counts(k):
        return remote(csend.at[k], cnts.at[k], cs.at[k], cr.at[k], at_offset(k, 1))

    def adjacent(k):
        return remote(docs.at[k], docs.at[32 + k], fs.at[k], fr.at[k], along_z(1))

    def further(k):
        return remote(docs.at[32 + k], docs.at[64 + k], gs.at[k], gr.at[k], along_z(1))

    def back(k):
        return remote(docs.at[k], docs.at[64 + k], gs.at[k], gr.at[k], along_z(3))

    def counts(i, to, h, target):
        return remote(cnts.at[pl.ds(8 * i, 8)], cnts.at[pl.ds(8 * to, 8)], hs.at[h], hr.at[h], target)

    def adjacent_counts(i):
        return counts(i, 4 + i, i, along_z(1))

    def further_counts(i):
        return counts(4 + i, 8 + i, 4 + i, along_z(1))

    def back_counts(i):
        return counts(2 + i, 10 + i, 6 + i, along_z(3))

    sends_further = (m == 1) | (m == 2)
    gets_further = m >= 2
    sends_back = m < 2
    gets_back = (m == 3) | (m == 0)

    def load(b):
        at = pl.ds(256 * b, 256)
        return pltpu.make_async_copy(emb_ref.at[at], emb.at[at], ls.at[b])

    for b in range(4):
        load(b).start()

    zrecv_a[...] = jnp.full_like(zrecv_a, -1.0)
    zrecv_f[...] = jnp.full_like(zrecv_f, -1.0)
    zrecv_b[...] = jnp.full_like(zrecv_b, -1.0)

    barrier = pltpu.get_barrier_semaphore()

    def greet(k, carry):
        pl.semaphore_signal(barrier, 1, device_id=at_offset(k, -1), device_id_type=MESH)
        return carry

    lax.fori_loop(1, 32, greet, 0)
    for d in (1, 2, 3):
        pl.semaphore_signal(barrier, 1, device_id=along_z(d), device_id_type=MESH)

    grp = grp_ref[...]
    gy, gx, gc = grp // 8, (grp // 2) & 3, grp & 1
    off = ((gy - y) & 3) * 8 + ((gx - x) & 3) * 2 + ((gc - c) & 1)
    place = (off * 3) & 31
    clu = clu_ref[...]
    kind = place * 2 + clu
    mine = (lax.broadcasted_iota(I32, (64, 1024), 0) == kind).astype(F32)
    mine_b = mine.astype(BF16)
    before = (
        lax.broadcasted_iota(I32, (256, 256), 0) < lax.broadcasted_iota(I32, (256, 256), 1)
    ).astype(F32).astype(BF16)
    offset = jnp.zeros((64, 1), F32)
    ranks = []
    for b in range(4):
        part = mine[:, 256 * b : 256 * b + 256]
        within = dot_nn(mine_b[:, 256 * b : 256 * b + 256], before) + offset
        ranks.append(jnp.sum(part * within, axis=0, keepdims=True))
        offset = offset + jnp.sum(part, axis=1, keepdims=True)
    rank = jnp.concatenate(ranks, axis=1).astype(I32)
    rank = jnp.where(clu == 0, rank, CAP - 1 - rank)
    slot = place * CAP + rank

    same = (lax.broadcasted_iota(I32, (256, 1024), 0) // 4 == kind).astype(F32)
    total = jnp.sum(same, axis=1, keepdims=True)
    csend[...] = jnp.broadcast_to(total, (256, 128)).reshape(32, 8, 128)

    row_best[...] = jnp.full_like(row_best, -1.0)
    col_best[...] = jnp.full_like(col_best, -1.0)

    for b in range(4):
        load(b).wait()
        rows = emb[256 * b : 256 * b + 256, :].astype(F32)
        norm = jnp.sqrt(jnp.sum(rows * rows, axis=1, keepdims=True) + 1e-06)
        unit[256 * b : 256 * b + 256, :] = (rows * (1.0 / norm)).astype(BF16)

    def start_first(k, carry):
        first_hop(k).start()
        first_counts(k).start()
        return carry

    for b in range(4):
        here = lax.broadcasted_iota(I32, (8 * CAP, 1024), 0) + 8 * CAP * b == slot
        picked = dot_nn(here.astype(F32).astype(BF16), unit[...]).astype(BF16)
        send[8 * b : 8 * b + 8] = picked.reshape(8, CAP, 1024)
        if b == 0:
            docs[0] = send[0]
            cnts[0] = csend[0]
            pl.semaphore_wait(barrier, 34)
        lax.fori_loop(max(1, 8 * b), 8 * b + 8, start_first, 0)

    def relay_further(k):
        adjacent(k).wait_recv()

        @pl.when(sends_further & (k < 16))
        def _():
            further(k).start()

    def relay(k, carry):
        @pl.when(k >= 1)
        def _():
            first_hop(k).wait_recv()
            first_counts(k).wait_recv()

        adjacent(k).start()

        @pl.when(sends_back & (k >= 16))
        def _():
            back(k).start()

        @pl.when(lax.rem(k, 8) == 7)
        def _():
            adjacent_counts(k // 8).start()

            @pl.when(sends_back & (k >= 16))
            def _():
                back_counts(k // 8 - 2).start()

        @pl.when(k >= LAG)
        def _():
            relay_further(k - LAG)

        return carry

    def late(k, carry):
        relay_further(k)
        return carry

    def wait_opposite(k, carry):
        further(k).wait_recv()
        return carry

    def prepare(r):
        lane_row = lax.broadcasted_iota(I32, (CAP, 128), 0).astype(F32)
        for k in range(8):
            n0 = cnts[8 * r + k, 0:1, :]
            n1 = cnts[8 * r + k, 4:5, :]
            lab = jnp.where(lane_row < n0, 0.0, jnp.where(lane_row >= CAP - n1, 1.0, -1.0))
            at = QUARTER * r + CAP * k
            lab_c[at : at + CAP, :] = lab
        if r < 8:
            for b in range(3):
                at = QUARTER * r + 128 * b
                lab_r[:, at : at + 128] = lab_c[at : at + 128, :].T[0:8, :]

    def lanes_of(r):
        for b in range(3):
            at = QUARTER * r + 128 * b
            rows_r[:, at : at + 128] = jnp.max(row_best[at : at + 128, :].T, axis=0, keepdims=True)

    def step(j, carry):
        lo, hi = pick(j, [0] + UNTIL), pick(j, UNTIL + [32])
        lax.fori_loop(lo, hi, relay, 0)

        def before(i, only=None):
            return pl.when(j == i if only is None else (j == i) & only)

        @before(0)
        def _():
            prepare(0)
            prepare(1)

        for i in (0, 1):

            @before(2 + i)
            def _(i=i):
                adjacent_counts(i).wait_recv()

                @pl.when(sends_further)
                def _():
                    further_counts(i).start()

                prepare(4 + i)

            @before((4, 6)[i], gets_further)
            def _(i=i):
                further_counts(i).wait_recv()
                lax.fori_loop(8 * i, 8 * i + 8, wait_opposite, 0)
                prepare(8 + i)

            @before((8, 20)[i], gets_back)
            def _(i=i):
                back_counts(i).wait_recv()
                lax.fori_loop(16 + 8 * i, 24 + 8 * i, wait_opposite, 0)
                prepare(10 + i)

        @before(5)
        def _():
            prepare(2)

        @before(7)
        def _():
            adjacent_counts(2).wait_recv()
            prepare(6)

        @before(9)
        def _():
            prepare(3)

        @before(17)
        def _():
            for r in range(7):
                lanes_of(r)

            @pl.when(gets_further)
            def _():
                for r in (8, 9):
                    lanes_of(r)
                zsend_f[...] = rows_r[:, 4 * HALF : 5 * HALF]
                to_far.start()

            lax.fori_loop(32 - LAG, 32, late, 0)
            adjacent_counts(3).wait_recv()
            prepare(7)

        r = pick(j, [0, 1, 4, 5, 8, 2, 9, 6, 10, 3, 2, 3, 4, 5, 8, 9, 6, 7, 7, 10, 11, 11])
        q = pick(j, [0, 0, 0, 0, 0, 0, 0, 0, 2, 0, 1, 1, 1, 1, 1, 1, 1, 0, 1, 3, 2, 3])
        wanted = (r < 8) | ((r < 10) & gets_further) | ((r >= 10) & gets_back)

        @pl.when(wanted)
        def _():
            left = docs[pl.ds(8 * r, 8)].reshape(QUARTER, 1024)
            right = docs[pl.ds(16 * q, 16)].reshape(HALF, 1024)
            sims[...] = dot_nt(left, right)

            @pl.when(r // 2 == q)
            def _():
                eye = lax.broadcasted_iota(I32, (128, 128), 0) == lax.broadcasted_iota(I32, (128, 128), 1)
                for b in range(3):
                    at = slice(128 * b, 128 * b + 128)
                    to = pl.ds(pl.multiple_of(QUARTER * lax.rem(r, 2) + 128 * b, 128), 128)
                    sims[at, to] = jnp.where(eye, -1.0, sims[at, to])

            r0 = pl.multiple_of(r * QUARTER, QUARTER)
            q0 = pl.multiple_of(q * HALF, HALF)
            labels = lab_c[pl.ds(r0, QUARTER), :]
            best = row_best[pl.ds(r0, QUARTER), :]
            for b in range(6):
                tile = sims[:, 128 * b : 128 * b + 128]
                cols = pl.ds(pl.multiple_of(q0 + 128 * b, 128), 128)
                tile = jnp.where(labels == lab_r[0:1, cols], tile, -1.0)
                best = jnp.maximum(best, tile)
                top = jnp.max(tile.reshape(QUARTER // 8, 8, 128), axis=0)
                col_best[:, cols] = jnp.maximum(col_best[:, cols], top)
            row_best[pl.ds(r0, QUARTER), :] = best

        return carry

    to_left = remote(zsend_a, zrecv_a, zs.at[0], zr.at[0], along_z(3))
    to_far = remote(zsend_f, zrecv_f, zs.at[1], zr.at[1], along_z(2))
    to_right = remote(zsend_b, zrecv_b, zs.at[2], zr.at[2], along_z(1))
    lax.fori_loop(0, TASKS, step, 0)

    def cols_of(h):
        return jnp.max(col_best[:, HALF * h : HALF * h + HALF], axis=0, keepdims=True)

    def both_of(h):
        return jnp.maximum(rows_r[:, HALF * h : HALF * h + HALF], cols_of(h))

    lanes_of(7)
    zsend_a[:, 0:HALF] = both_of(2)
    zsend_a[:, HALF : 2 * HALF] = both_of(3)
    to_left.start()

    @pl.when(gets_back)
    def _():
        lanes_of(10)
        lanes_of(11)
        zsend_b[...] = rows_r[:, 5 * HALF : 6 * HALF]
        to_right.start()

    res[:, 2 * HALF :] = jnp.full((1, 128), -1.0, F32)
    res[:, 0:HALF] = both_of(0)
    res[:, HALF : 2 * HALF] = both_of(1)

    @pl.when(m < 2)
    def _():
        to_far.wait_recv()
        to_right.wait_recv()

    to_left.wait_recv()
    others = jnp.concatenate([zrecv_f[...], zrecv_b[...]], axis=1)
    others = jnp.maximum(others, zrecv_a[...])
    res[:, 0 : 2 * HALF] = jnp.maximum(res[:, 0 : 2 * HALF], others)

    def answer(k):
        at = CAP * k // 128 * 128
        return remote(res.at[:, pl.ds(at, 256)], ret.at[k], rs.at[k], rr.at[k], at_offset(k, -1))

    for k in range(1, 32):
        answer(k).start()
    ret[0] = res[:, 0:256]

    def sent(k, carry):
        @pl.when(k >= 1)
        def _():
            first_hop(k).wait_send()
            first_counts(k).wait_send()

        adjacent(k).wait_send()

        @pl.when(sends_further & (k < 16))
        def _():
            further(k).wait_send()

        @pl.when(sends_back & (k >= 16))
        def _():
            back(k).wait_send()

        return carry

    lax.fori_loop(0, 32, sent, 0)
    for i in range(4):
        adjacent_counts(i).wait_send()
    to_left.wait_send()

    @pl.when(sends_further)
    def _():
        for i in (0, 1):
            further_counts(i).wait_send()

    @pl.when(sends_back)
    def _():
        for i in (0, 1):
            back_counts(i).wait_send()

    @pl.when(gets_further)
    def _():
        to_far.wait_send()

    @pl.when(gets_back)
    def _():
        to_right.wait_send()

    for k in range(1, 32):
        answer(k).wait_recv()
        answer(k).wait_send()
    table = jnp.concatenate([ret[k] for k in range(32)], axis=0)
    where = (lax.broadcasted_iota(I32, (32, 1024), 0) == place).astype(F32).astype(BF16)
    high = table.astype(BF16)
    rest = table - high.astype(F32)
    mid = rest.astype(BF16)
    low = (rest - mid.astype(F32)).astype(BF16)
    found = dot_tn(high, where) + dot_tn(mid, where) + dot_tn(low, where)
    lane = rank + ((place * CAP) & 127)
    hit = lax.broadcasted_iota(I32, (256, 1024), 0) == lane
    out_ref[...] = jnp.max(jnp.where(hit, found, -2.0), axis=0, keepdims=True)


def per_device(embeddings, doc_group, doc_cluster):
    vmem = pl.BlockSpec(memory_space=pltpu.VMEM)
    dma = pltpu.SemaphoreType.DMA
    out = pl.pallas_call(
        kernel,
        out_shape=jax.ShapeDtypeStruct((1, 1024), F32),
        in_specs=[pl.BlockSpec(memory_space=pl.ANY), vmem, vmem],
        out_specs=vmem,
        scratch_shapes=[
            pltpu.VMEM((1024, 1024), BF16),
            pltpu.VMEM((1024, 1024), BF16),
            pltpu.VMEM((32, CAP, 1024), BF16),
            pltpu.VMEM((32, 8, 128), F32),
            pltpu.VMEM((96, CAP, 1024), BF16),
            pltpu.VMEM((96, 8, 128), F32),
            pltpu.VMEM((6 * HALF, 128), F32),
            pltpu.VMEM((8, 4 * HALF), F32),
            pltpu.VMEM((QUARTER, HALF), F32),
            pltpu.VMEM((6 * HALF, 128), F32),
            pltpu.VMEM((8, 4 * HALF), F32),
            pltpu.VMEM((1, 6 * HALF), F32),
            pltpu.VMEM((1, 2 * HALF), F32),
            pltpu.VMEM((1, HALF), F32),
            pltpu.VMEM((1, HALF), F32),
            pltpu.VMEM((1, 2 * HALF), F32),
            pltpu.VMEM((1, HALF), F32),
            pltpu.VMEM((1, HALF), F32),
            pltpu.VMEM((1, 2 * HALF + 128), F32),
            pltpu.VMEM((32, 1, 256), F32),
            dma((4,)), dma((32,)), dma((32,)), dma((32,)), dma((32,)),
            dma((32,)), dma((32,)), dma((32,)), dma((32,)),
            dma((8,)), dma((8,)), dma((3,)), dma((3,)), dma((32,)), dma((32,)),
        ],
        compiler_params=pltpu.CompilerParams(
            collective_id=0, has_side_effects=True, vmem_limit_bytes=56 << 20
        ),
        cost_estimate=pl.CostEstimate(flops=24_000_000_000, bytes_accessed=2_200_000, transcendentals=0),
    )(embeddings, doc_group.reshape(1, -1), doc_cluster.reshape(1, -1))
    return out.reshape(-1)


def solution(mesh):
    in_specs = (P(("grp", "blk"), None), P(("grp", "blk"), None), P(("grp", "blk")))
    out_specs = P(("grp", "blk"))
    return jax.shard_map(
        per_device, mesh=mesh, in_specs=in_specs, out_specs=out_specs, check_vma=False
    )
```

```python
import functools

import jax
import jax.numpy as jnp
from jax import lax
from jax.experimental import pallas as pl
from jax.experimental.pallas import tpu as pltpu
from jax.sharding import PartitionSpec as P

MESH = pl.DeviceIdType.MESH
F32, BF16, I32 = jnp.float32, jnp.bfloat16, jnp.int32
GROUPS, CAP = 32, 48
HALF = 16 * CAP
LAG = 7
QUARTER = 8 * CAP
ORDER = [
    (0, 0, 16), (1, 0, 17), (4, 0, 19), (5, 0, 23), (8, 0, 24), (2, 0, 25),
    (9, 0, 27), (6, 0, 31), (10, 2, 32), (3, 0, 32), (2, 1, 32), (3, 1, 32),
    (4, 1, 32), (5, 1, 32), (8, 1, 32), (9, 1, 32), (6, 1, 32), (7, 0, 32),
    (7, 1, 32), (10, 3, 32), (11, 2, 32), (11, 3, 32),
]
TASKS = len(ORDER)
OFFSETS = [
    0, 1, 6, 30, 18, 2, 8, 7, 31, 19, 3, 9, 12, 14, 16, 26,
    4, 13, 15, 17, 27, 5, 24, 10, 20, 28, 22, 25, 11, 21, 29, 23,
]
AT = {(r, q): j for j, (r, q, _) in reversed(list(enumerate(ORDER)))}


def dot_nt(a, b):
    return lax.dot_general(a, b, (((1,), (1,)), ((), ())), preferred_element_type=F32)


def dot_nn(a, b):
    return lax.dot_general(a, b, (((1,), (0,)), ((), ())), preferred_element_type=F32)


def dot_tn(a, b):
    return lax.dot_general(a, b, (((0,), (0,)), ((), ())), preferred_element_type=F32)


def pick(index, values):
    out = values[-1]
    for i in range(len(values) - 2, -1, -1):
        out = jnp.where(index == i, values[i], out)
    return out


def kernel(
    emb_ref, grp_ref, clu_ref, out_ref,
    emb, unit, send, csend, docs, cnts, lab_c, lab_r, sims, row_best, col_best,
    rows_r, zsend_a, zsend_f, zsend_b, zrecv_a, zrecv_f, zrecv_b, res, ret,
    ls, ss, sr, cs, cr, fs, fr, gs, gr, hs, hr, zs, zr, rs, rr,
):
    g = lax.axis_index("grp")
    z = lax.axis_index("blk")
    y, x, c = g // 8, lax.rem(g // 2, 4), lax.rem(g, 2)
    m = jnp.where(c == 0, z, lax.rem(4 - z, 4))

    def along_z(d):
        return (g, lax.rem(z + jnp.where(c == 0, d, 4 - d), 4))

    def at_offset(k, sign):
        off = OFFSETS[k]
        dy, dx, dc = off // 8, off // 2 % 4, off % 2
        ty, tx = lax.rem(y + 4 + sign * dy, 4), lax.rem(x + 4 + sign * dx, 4)
        return ((ty * 4 + tx) * 2 + lax.rem(c + dc, 2), z)

    def remote(src, dst, s_sem, r_sem, target):
        return pltpu.make_async_remote_copy(
            src_ref=src, dst_ref=dst, send_sem=s_sem, recv_sem=r_sem,
            device_id=target, device_id_type=MESH,
        )

    def first_hop(k):
        to = at_offset(k, 1) if isinstance(k, int) else along_z(1)
        return remote(send.at[k], docs.at[k], ss.at[k], sr.at[k], to)

    def first_counts(k):
        to = at_offset(k, 1) if isinstance(k, int) else along_z(1)
        return remote(csend.at[k], cnts.at[k], cs.at[k], cr.at[k], to)

    def adjacent(k):
        return remote(docs.at[k], docs.at[32 + k], fs.at[k], fr.at[k], along_z(1))

    def further(k):
        return remote(docs.at[32 + k], docs.at[64 + k], gs.at[k], gr.at[k], along_z(1))

    def back(k):
        return remote(docs.at[k], docs.at[64 + k], gs.at[k], gr.at[k], along_z(3))

    def counts(i, to, h, target):
        return remote(cnts.at[pl.ds(8 * i, 8)], cnts.at[pl.ds(8 * to, 8)], hs.at[h], hr.at[h], target)

    def adjacent_counts(i):
        return counts(i, 4 + i, i, along_z(1))

    def further_counts(i):
        return counts(4 + i, 8 + i, 4 + i, along_z(1))

    def back_counts(i):
        return counts(2 + i, 10 + i, 6 + i, along_z(3))

    sends_further = (m == 1) | (m == 2)
    gets_further = m >= 2
    sends_back = m < 2
    gets_back = (m == 3) | (m == 0)

    def load(b):
        at = pl.ds(256 * b, 256)
        return pltpu.make_async_copy(emb_ref.at[at], emb.at[at], ls.at[b])

    for b in range(4):
        load(b).start()

    zrecv_a[...] = jnp.full_like(zrecv_a, -1.0)
    zrecv_f[...] = jnp.full_like(zrecv_f, -1.0)
    zrecv_b[...] = jnp.full_like(zrecv_b, -1.0)

    barrier = pltpu.get_barrier_semaphore()

    def greet(k, carry):
        pl.semaphore_signal(barrier, 1, device_id=at_offset(k, -1), device_id_type=MESH)
        return carry

    for k in range(1, 32):
        greet(k, 0)
    for d in (1, 2, 3):
        pl.semaphore_signal(barrier, 1, device_id=along_z(d), device_id_type=MESH)

    grp = grp_ref[...]
    gy, gx, gc = grp // 8, (grp // 2) & 3, grp & 1
    off = ((gy - y) & 3) * 8 + ((gx - x) & 3) * 2 + ((gc - c) & 1)
    place = jnp.zeros_like(off)
    for k in range(1, 32):
        place = jnp.where(off == OFFSETS[k], k, place)
    clu = clu_ref[...]
    kind = place * 2 + clu
    mine = (lax.broadcasted_iota(I32, (64, 1024), 0) == kind).astype(F32)
    mine_b = mine.astype(BF16)
    before = (
        lax.broadcasted_iota(I32, (256, 256), 0) < lax.broadcasted_iota(I32, (256, 256), 1)
    ).astype(F32).astype(BF16)
    offset = jnp.zeros((64, 1), F32)
    ranks = []
    for b in range(4):
        part = mine[:, 256 * b : 256 * b + 256]
        within = dot_nn(mine_b[:, 256 * b : 256 * b + 256], before) + offset
        ranks.append(jnp.sum(part * within, axis=0, keepdims=True))
        offset = offset + jnp.sum(part, axis=1, keepdims=True)
    rank = jnp.concatenate(ranks, axis=1).astype(I32)
    rank = jnp.where(clu == 0, rank, CAP - 1 - rank)
    slot = place * CAP + rank

    same = (lax.broadcasted_iota(I32, (256, 1024), 0) // 4 == kind).astype(F32)
    total = jnp.sum(same, axis=1, keepdims=True)
    csend[...] = jnp.broadcast_to(total, (256, 128)).reshape(32, 8, 128)

    row_best[...] = jnp.full_like(row_best, -1.0)
    col_best[...] = jnp.full_like(col_best, -1.0)

    for b in range(4):
        load(b).wait()
        rows = emb[256 * b : 256 * b + 256, :].astype(F32)
        norm = jnp.sqrt(jnp.sum(rows * rows, axis=1, keepdims=True) + 1e-06)
        unit[256 * b : 256 * b + 256, :] = (rows * (1.0 / norm)).astype(BF16)

    for b in range(4):
        here = lax.broadcasted_iota(I32, (8 * CAP, 1024), 0) + 8 * CAP * b == slot
        picked = dot_nn(here.astype(F32).astype(BF16), unit[...]).astype(BF16)
        send[8 * b : 8 * b + 8] = picked.reshape(8, CAP, 1024)
        if b == 0:
            docs[0] = send[0]
            cnts[0] = csend[0]
            pl.semaphore_wait(barrier, 34)
        for k in range(max(1, 8 * b), 8 * b + 8):
            first_hop(k).start()
            first_counts(k).start()

    def relay_further(k):
        adjacent(k).wait_recv()

        @pl.when(sends_further & (k < 16))
        def _():
            further(k).start()

    def relay(k, carry):
        @pl.when(k >= 1)
        def _():
            first_hop(k).wait_recv()
            first_counts(k).wait_recv()

        adjacent(k).start()

        @pl.when(sends_back & (k >= 16))
        def _():
            back(k).start()

        @pl.when(lax.rem(k, 8) == 7)
        def _():
            adjacent_counts(k // 8).start()

            @pl.when(sends_back & (k >= 16))
            def _():
                back_counts(k // 8 - 2).start()

        @pl.when((k >= LAG) & (k < LAG + 16))
        def _():
            relay_further(k - LAG)

        return carry

    def late(k, carry):
        relay_further(k)
        return carry

    def wait_opposite(k, carry):
        further(k).wait_recv()
        return carry

    def prepare(r):
        lane_row = lax.broadcasted_iota(I32, (CAP, 128), 0).astype(F32)
        for k in range(8):
            n0 = cnts[8 * r + k, 0:1, :]
            n1 = cnts[8 * r + k, 4:5, :]
            lab = jnp.where(lane_row < n0, 0.0, jnp.where(lane_row >= CAP - n1, 1.0, -1.0))
            at = QUARTER * r + CAP * k
            lab_c[at : at + CAP, :] = lab
        if r < 8:
            for b in range(3):
                at = QUARTER * r + 128 * b
                lab_r[:, at : at + 128] = lab_c[at : at + 128, :].T[0:8, :]

    def lanes_of(r):
        for b in range(3):
            at = QUARTER * r + 128 * b
            rows_r[:, at : at + 128] = jnp.max(row_best[at : at + 128, :].T, axis=0, keepdims=True)

    def step(j, carry):
        until = [u for _, _, u in ORDER]
        lax.fori_loop(pick(j, [0] + until[:-1]), pick(j, until), relay, 0)

        def before(i, only=None):
            return pl.when(j == i if only is None else (j == i) & only)

        @before(AT[0, 0])
        def _():
            prepare(0)
            prepare(1)

        for i in (0, 1):

            @before(AT[4 + i, 0])
            def _(i=i):
                adjacent_counts(i).wait_recv()

                @pl.when(sends_further)
                def _():
                    further_counts(i).start()

                prepare(4 + i)

            @before(AT[8 + i, 0], gets_further)
            def _(i=i):
                further_counts(i).wait_recv()
                lax.fori_loop(8 * i, 8 * i + 8, wait_opposite, 0)
                prepare(8 + i)

            @before(AT[10 + i, 2], gets_back)
            def _(i=i):
                back_counts(i).wait_recv()
                lax.fori_loop(16 + 8 * i, 24 + 8 * i, wait_opposite, 0)
                prepare(10 + i)

        @before(AT[2, 0])
        def _():
            prepare(2)

        @before(AT[6, 0])
        def _():
            lax.fori_loop(16, 24, late, 0)
            adjacent_counts(2).wait_recv()
            prepare(6)

        @before(AT[3, 0])
        def _():
            prepare(3)

        @before(AT[7, 0])
        def _():
            for r in range(7):
                lanes_of(r)

            @pl.when(gets_further)
            def _():
                for r in (8, 9):
                    lanes_of(r)
                zsend_f[...] = rows_r[:, 4 * HALF : 5 * HALF]
                to_far.start()

            lax.fori_loop(24, 32, late, 0)
            adjacent_counts(3).wait_recv()
            prepare(7)

        r = pick(j, [r for r, _, _ in ORDER])
        q = pick(j, [q for _, q, _ in ORDER])
        wanted = (r < 8) | ((r < 10) & gets_further) | ((r >= 10) & gets_back)

        @pl.when(wanted)
        def _():
            left = docs[pl.ds(8 * r, 8)].reshape(QUARTER, 1024)
            right = docs[pl.ds(16 * q, 16)].reshape(HALF, 1024)
            sims[...] = dot_nt(left, right)

            @pl.when(r // 2 == q)
            def _():
                eye = lax.broadcasted_iota(I32, (128, 128), 0) == lax.broadcasted_iota(I32, (128, 128), 1)
                for b in range(3):
                    at = slice(128 * b, 128 * b + 128)
                    to = pl.ds(pl.multiple_of(QUARTER * lax.rem(r, 2) + 128 * b, 128), 128)
                    sims[at, to] = jnp.where(eye, -1.0, sims[at, to])

            r0 = pl.multiple_of(r * QUARTER, QUARTER)
            q0 = pl.multiple_of(q * HALF, HALF)
            labels = lab_c[pl.ds(r0, QUARTER), :]
            best = row_best[pl.ds(r0, QUARTER), :]
            for b in range(6):
                tile = sims[:, 128 * b : 128 * b + 128]
                cols = pl.ds(pl.multiple_of(q0 + 128 * b, 128), 128)
                tile = jnp.where(labels == lab_r[0:1, cols], tile, -1.0)
                best = jnp.maximum(best, tile)
                top = jnp.max(tile.reshape(QUARTER // 8, 8, 128), axis=0)
                col_best[:, cols] = jnp.maximum(col_best[:, cols], top)
            row_best[pl.ds(r0, QUARTER), :] = best

        return carry

    to_left = remote(zsend_a, zrecv_a, zs.at[0], zr.at[0], along_z(3))
    to_far = remote(zsend_f, zrecv_f, zs.at[1], zr.at[1], along_z(2))
    to_right = remote(zsend_b, zrecv_b, zs.at[2], zr.at[2], along_z(1))
    lax.fori_loop(0, TASKS, step, 0)

    def cols_of(h):
        return jnp.max(col_best[:, HALF * h : HALF * h + HALF], axis=0, keepdims=True)

    def both_of(h):
        return jnp.maximum(rows_r[:, HALF * h : HALF * h + HALF], cols_of(h))

    lanes_of(7)
    zsend_a[:, 0:HALF] = both_of(2)
    zsend_a[:, HALF : 2 * HALF] = both_of(3)
    to_left.start()

    @pl.when(gets_back)
    def _():
        lanes_of(10)
        lanes_of(11)
        zsend_b[...] = rows_r[:, 5 * HALF : 6 * HALF]
        to_right.start()

    res[:, 2 * HALF :] = jnp.full((1, 128), -1.0, F32)
    res[:, 0:HALF] = both_of(0)
    res[:, HALF : 2 * HALF] = both_of(1)

    @pl.when(m < 2)
    def _():
        to_far.wait_recv()
        to_right.wait_recv()

    to_left.wait_recv()
    others = jnp.concatenate([zrecv_f[...], zrecv_b[...]], axis=1)
    others = jnp.maximum(others, zrecv_a[...])
    res[:, 0 : 2 * HALF] = jnp.maximum(res[:, 0 : 2 * HALF], others)

    def answer(k):
        at = CAP * k // 128 * 128
        return remote(res.at[:, pl.ds(at, 256)], ret.at[k], rs.at[k], rr.at[k], at_offset(k, -1))

    for k in range(1, 32):
        answer(k).start()
    ret[0] = res[:, 0:256]

    def sent(k, carry):
        @pl.when(k >= 1)
        def _():
            first_hop(k).wait_send()
            first_counts(k).wait_send()

        adjacent(k).wait_send()

        @pl.when(sends_further & (k < 16))
        def _():
            further(k).wait_send()

        @pl.when(sends_back & (k >= 16))
        def _():
            back(k).wait_send()

        return carry

    lax.fori_loop(0, 32, sent, 0)
    for i in range(4):
        adjacent_counts(i).wait_send()
    to_left.wait_send()

    @pl.when(sends_further)
    def _():
        for i in (0, 1):
            further_counts(i).wait_send()

    @pl.when(sends_back)
    def _():
        for i in (0, 1):
            back_counts(i).wait_send()

    @pl.when(gets_further)
    def _():
        to_far.wait_send()

    @pl.when(gets_back)
    def _():
        to_right.wait_send()

    for k in range(1, 32):
        answer(k).wait_recv()
        answer(k).wait_send()
    table = jnp.concatenate([ret[k] for k in range(32)], axis=0)
    where = (lax.broadcasted_iota(I32, (32, 1024), 0) == place).astype(F32).astype(BF16)
    high = table.astype(BF16)
    rest = table - high.astype(F32)
    mid = rest.astype(BF16)
    low = (rest - mid.astype(F32)).astype(BF16)
    found = dot_tn(high, where) + dot_tn(mid, where) + dot_tn(low, where)
    lane = rank + ((place * CAP) & 127)
    hit = lax.broadcasted_iota(I32, (256, 1024), 0) == lane
    out_ref[...] = jnp.max(jnp.where(hit, found, -2.0), axis=0, keepdims=True)


def per_device(embeddings, doc_group, doc_cluster):
    vmem = pl.BlockSpec(memory_space=pltpu.VMEM)
    dma = pltpu.SemaphoreType.DMA
    out = pl.pallas_call(
        kernel,
        out_shape=jax.ShapeDtypeStruct((1, 1024), F32),
        in_specs=[pl.BlockSpec(memory_space=pl.ANY), vmem, vmem],
        out_specs=vmem,
        scratch_shapes=[
            pltpu.VMEM((1024, 1024), BF16),
            pltpu.VMEM((1024, 1024), BF16),
            pltpu.VMEM((32, CAP, 1024), BF16),
            pltpu.VMEM((32, 8, 128), F32),
            pltpu.VMEM((96, CAP, 1024), BF16),
            pltpu.VMEM((96, 8, 128), F32),
            pltpu.VMEM((6 * HALF, 128), F32),
            pltpu.VMEM((8, 4 * HALF), F32),
            pltpu.VMEM((QUARTER, HALF), F32),
            pltpu.VMEM((6 * HALF, 128), F32),
            pltpu.VMEM((8, 4 * HALF), F32),
            pltpu.VMEM((1, 6 * HALF), F32),
            pltpu.VMEM((1, 2 * HALF), F32),
            pltpu.VMEM((1, HALF), F32),
            pltpu.VMEM((1, HALF), F32),
            pltpu.VMEM((1, 2 * HALF), F32),
            pltpu.VMEM((1, HALF), F32),
            pltpu.VMEM((1, HALF), F32),
            pltpu.VMEM((1, 2 * HALF + 128), F32),
            pltpu.VMEM((32, 1, 256), F32),
            dma((4,)), dma((32,)), dma((32,)), dma((32,)), dma((32,)),
            dma((32,)), dma((32,)), dma((32,)), dma((32,)),
            dma((8,)), dma((8,)), dma((3,)), dma((3,)), dma((32,)), dma((32,)),
        ],
        compiler_params=pltpu.CompilerParams(
            collective_id=0, has_side_effects=True, vmem_limit_bytes=56 << 20
        ),
        cost_estimate=pl.CostEstimate(flops=24_000_000_000, bytes_accessed=2_200_000, transcendentals=0),
    )(embeddings, doc_group.reshape(1, -1), doc_cluster.reshape(1, -1))
    return out.reshape(-1)


def solution(mesh):
    in_specs = (P(("grp", "blk"), None), P(("grp", "blk"), None), P(("grp", "blk")))
    out_specs = P(("grp", "blk"))
    return jax.shard_map(
        per_device, mesh=mesh, in_specs=in_specs, out_specs=out_specs, check_vma=False
    )
```
